32 devices in a mesh: dp: 8 (over z, x), mp: 4 (over y, core).
Axes of the slice: x: 2, y: 2, z: 4, core: 2. Of those that a mesh axis runs over, the one named last changes fastest.
Arguments:
- grad_out: bfloat16 [2048, 3072], P(('dp', 'mp')), may hold values from -6 to 6
- attn_out: bfloat16 [2048, 4096], P('dp', 'mp'), may hold values from -6 to 6
- weight_codes: bfloat16 [4096, 3072], P('mp', 'dp'), may hold values from -6 to 6
- block_scales: bfloat16 [128, 3072], P('mp', 'dp'), may hold values from 0.0029907227 to 0.049804688
Outputs:
- grad_attn: bfloat16 [2048, 4096], P('dp', 'mp')
- grad_weight_t: bfloat16 [3072, 4096], P('dp', 'mp')
The draws below stay inside these ranges and needn't reach their ends.
All inputs are finite; a program needn't handle non-finite values.
Results may differ from the reference program's by a relative error of at most 0.0049.
Values may be sent and summed in bfloat16 or wider, within the bound.
No kernel may reach another device: no remote copies, remote signals or barrier semaphores. Data moves between devices by JAX's collectives and lax.ppermute only.
A program may use at most 64 MiB of HBM per device.

```python
import math
import jax
import jax.numpy as jnp
from jax import lax

D = 3072
BLOCK = 32
HD = 4096
GROUP = 256
TOKENS = 2048
N_DP = 8


def strengthened(array, stream_key, source, target, parts, factor):
    def block_of(axis_at):
        return (jnp.arange(array.shape[axis_at]) // (array.shape[axis_at] // parts)).reshape((-1,) + (1,) * (array.ndim - 1 - axis_at))

    near = jax.random.permutation(stream_key, parts)[block_of(target)]
    other_side = (block_of(target) + parts // 2) % parts
    return jnp.where((block_of(source) == near) | (block_of(source) == other_side), factor * array, array)


def levels(key, extent, cuts, low, high):
    loudness = 1.0
    for axis_at, blocks in cuts:
        heights = jax.random.uniform(jax.random.fold_in(jax.random.fold_in(key, 6), axis_at), (blocks,), jnp.float32, low / len(cuts), high / len(cuts))
        loudness = loudness * jnp.repeat(jnp.exp(heights), extent[axis_at] // blocks).reshape((-1,) + (1,) * (len(extent) - 1 - axis_at))
    return loudness


def centred(rng, extent, deviation, most, split=(), kind=jnp.bfloat16):
    values = deviation * jax.random.normal(rng, extent, jnp.float32)
    if split:
        values = values * levels(rng, extent, split, -0.22, 0.18)
    return jnp.clip(values, -most, most).astype(kind)


def bell_draw_with(own_key, extent, spread, bound, shards, heavy, held_as=jnp.bfloat16):
    drawn = spread * jax.random.normal(own_key, extent, jnp.float32)
    if shards:
        drawn = drawn * levels(own_key, extent, shards, -0.22, 0.18)
    return jnp.clip(strengthened(drawn, jax.random.fold_in(own_key, 3), *heavy), -bound, bound).astype(held_as)


def setup_inputs(seed: int = 0) -> dict:
    key_list = jax.random.split(jax.random.key(seed), 5)
    grad_out = bell_draw_with(key_list[0], (TOKENS, D), 1.0, 6.0, ((0, 32),), (0, 1, 32, 2.75))
    attn_out = centred(key_list[1], (TOKENS, HD), 1.0, 6.0, ((0, 8), (1, 4)))
    weight_codes = centred(key_list[2], (HD, D), 1.0, 6.0, ((0, 4), (1, 8)))
    block_scales = jnp.clip(jnp.exp(math.log(0.049804688) - 2.8125941 * jax.random.uniform(key_list[3], (HD // BLOCK, D), jnp.float32) ** levels(key_list[3], (HD // BLOCK, D), ((0, 4), (1, 8)), -0.2, 0.2)), 0.0029907227, 0.049804688).astype(jnp.bfloat16)
    return {"grad_out": grad_out, "attn_out": attn_out, "weight_codes": weight_codes, "block_scales": block_scales}


def reference(grad_out, attn_out, weight_codes, block_scales):
    expanded = jnp.repeat(block_scales.astype(jnp.float32), BLOCK, axis=0)
    weight = (weight_codes.astype(jnp.float32) * expanded).astype(jnp.bfloat16)
    grad_attn = jnp.dot(grad_out, weight.T, preferred_element_type=jnp.float32).astype(jnp.bfloat16)
    scaling = 1.0 / (float(TOKENS) ** 0.5)
    grad_groups = grad_out.reshape(N_DP, GROUP, D)
    attn_groups = attn_out.reshape(N_DP, GROUP, HD)

    def add_group(total, pieces):
        grad_piece, attn_piece = pieces
        partial_sum = jnp.dot(grad_piece.T, attn_piece, preferred_element_type=jnp.float32)
        return total + partial_sum * scaling, None

    total, unused = lax.scan(add_group, jnp.zeros((D, HD), jnp.float32), (grad_groups, attn_groups))
    return grad_attn, total.astype(jnp.bfloat16)
```

```python
import math

import jax
import jax.numpy as jnp
from jax import lax
from jax.sharding import PartitionSpec as P

BLOCK = 32
PAIR = 2


def dequantize(codes_part, scales_part):
    expanded = jnp.repeat(scales_part.astype(jnp.float32), BLOCK, axis=0)
    return (codes_part.astype(jnp.float32) * expanded).astype(jnp.bfloat16)


def by_own_bits(blocks, place, first_axis, count):
    for k in range(count):
        axis = first_axis + k
        bit = (place >> (count - 1 - k)) & 1
        blocks = jnp.where(bit == 1, jnp.flip(blocks, axis), blocks)
    return blocks


def halves(own, other, side, axis):
    first = jnp.where(side == 0, own, other)
    second = jnp.where(side == 0, other, own)
    return jnp.concatenate([first, second], axis)


def body(grad_out, attn_out, weight_codes, block_scales):
    n_dp, n_mp = lax.axis_size("dp"), lax.axis_size("mp")
    layers = n_dp // PAIR
    bits = n_mp.bit_length() - 1
    rows, features = grad_out.shape
    group_rows, heads = attn_out.shape
    own_features = weight_codes.shape[1]
    half = heads // PAIR
    layer_features = PAIR * own_features
    scaling = 1.0 / math.sqrt(group_rows * n_dp)

    dp, mp = lax.axis_index("dp"), lax.axis_index("mp")
    layer, side = dp // PAIR, dp % PAIR

    across = [(i, i ^ 1) for i in range(n_dp)]

    def layer_moves(step, keep=lambda z: True):
        return [
            (z * PAIR + x, (z + step) * PAIR + x)
            for z in range(layers)
            for x in range(PAIR)
            if 0 <= z + step < layers and keep(z)
        ]

    def swap_x(piece):
        return lax.ppermute(piece, "dp", across)

    def swap_mp(piece, bit):
        return lax.ppermute(piece, "mp", [(i, i ^ bit) for i in range(n_mp)])

    slots = []
    for r in range(layers):
        piece = lax.dynamic_slice_in_dim(
            grad_out, ((layer + r) % layers) * layer_features, layer_features, 1
        )
        if r:
            piece = lax.ppermute(
                piece,
                "dp",
                [
                    (z * PAIR + x, ((z + r) % layers) * PAIR + x)
                    for z in range(layers)
                    for x in range(PAIR)
                ],
            )
        slots.append(piece)
    own = jnp.stack(slots)

    by_token = attn_out.reshape((2,) * bits + (rows, heads))
    by_token = by_own_bits(by_token, mp, 0, bits).reshape(group_rows, heads)
    attn_own = lax.dynamic_slice_in_dim(by_token, side * half, half, 1)
    attn_other = swap_x(lax.dynamic_slice_in_dim(by_token, (1 - side) * half, half, 1))
    attn_layer = jnp.concatenate([attn_own, attn_other], 0)

    weight = dequantize(weight_codes, block_scales)
    weight_own = lax.dynamic_slice_in_dim(weight, side * half, half, 0)
    weight_other = swap_x(lax.dynamic_slice_in_dim(weight, (1 - side) * half, half, 0))
    weight_slab = halves(weight_own, weight_other, side, 1)

    top = n_mp // 2
    via_x = swap_x(own)
    via_mp = swap_mp(own, top)
    mixed = []
    for i in range(n_dp):
        for j in range(n_mp):
            there = ((i ^ 1), j) if j % 2 == 0 else (i, j ^ top)
            mixed.append((i * n_mp + j, there[0] * n_mp + there[1]))
    far = lax.ppermute(jnp.where(mp % 2 == 0, via_mp, via_x), ("dp", "mp"), mixed)
    gathered = jnp.stack([jnp.stack([own, via_mp], 1), jnp.stack([via_x, far], 1)], 1)
    for k in range(1, bits):
        bit = top >> k
        gathered = jnp.stack([gathered, swap_mp(gathered, bit)], 2 + k)
    layer_rows = PAIR * group_rows
    columns = gathered.reshape(layers, layer_rows, layer_features)

    up, down = [attn_layer], [attn_layer]
    for r in range(1, layers):
        up.append(lax.ppermute(up[-1], "dp", layer_moves(1, lambda z: z >= r - 1)))
        down.append(lax.ppermute(down[-1], "dp", layer_moves(-1, lambda z: z <= layers - r)))
    total = None
    for r in range(layers):
        rows_r = attn_layer if r == 0 else jnp.where(layer >= r, up[r], down[layers - r])
        term = lax.dot_general(
            columns[r], rows_r, (((0,), (0,)), ((), ())), preferred_element_type=jnp.float32
        )
        total = term if total is None else total + term
    gw = (scaling * total).astype(jnp.bfloat16)
    gw_own = lax.dynamic_slice_in_dim(gw, side * own_features, own_features, 0)
    gw_other = swap_x(lax.dynamic_slice_in_dim(gw, (1 - side) * own_features, own_features, 0))
    grad_weight_t = halves(gw_own, gw_other, side, 1)

    def terms(r):
        return lax.dot_general(
            columns[r], weight_slab, (((1,), (1,)), ((), ())), preferred_element_type=jnp.float32
        )

    parts = [terms(r) for r in range(layers)]
    from_below = from_above = None
    for k in range(1, layers):
        send_up, send_down = parts[k], parts[layers - k]
        if k > 1:
            send_up = send_up + from_below.astype(jnp.float32)
            send_down = send_down + from_above.astype(jnp.float32)
        from_below = lax.ppermute(
            send_up.astype(jnp.bfloat16), "dp", layer_moves(1, lambda z: z <= k - 1)
        )
        from_above = lax.ppermute(
            send_down.astype(jnp.bfloat16), "dp", layer_moves(-1, lambda z: z >= layers - k)
        )
    ga = parts[0] + from_below.astype(jnp.float32) + from_above.astype(jnp.float32)
    ga = ga.astype(jnp.bfloat16)
    ga_other = swap_x(ga[group_rows:])
    grad_attn = halves(ga[:group_rows], ga_other, side, 1)
    grad_attn = by_own_bits(grad_attn.reshape((2,) * bits + (rows, heads)), mp, 0, bits)
    return grad_attn.reshape(group_rows, heads), grad_weight_t


def solution(mesh):
    placed = (P(("dp", "mp"), None), P("dp", "mp"), P("mp", "dp"), P("mp", "dp"))
    return jax.shard_map(
        body, mesh=mesh, in_specs=placed, out_specs=(P("dp", "mp"), P("dp", "mp")), check_vma=False
    )
```

```python
import math

import jax
import jax.numpy as jnp
from jax import lax
from jax.sharding import PartitionSpec as P

BLOCK = 32
PAIR = 2


def dequantize(codes_part, scales_part):
    expanded = jnp.repeat(scales_part.astype(jnp.float32), BLOCK, axis=0)
    return (codes_part.astype(jnp.float32) * expanded).astype(jnp.bfloat16)


def by_own_bits(blocks, place, first_axis, count):
    for k in range(count):
        axis = first_axis + k
        bit = (place >> (count - 1 - k)) & 1
        blocks = jnp.where(bit == 1, jnp.flip(blocks, axis), blocks)
    return blocks


def halves(own, other, side, axis):
    first = jnp.where(side == 0, own, other)
    second = jnp.where(side == 0, other, own)
    return jnp.concatenate([first, second], axis)


def body(grad_out, attn_out, weight_codes, block_scales):
    n_dp, n_mp = lax.axis_size("dp"), lax.axis_size("mp")
    layers = n_dp // PAIR
    bits = n_mp.bit_length() - 1
    rows, features = grad_out.shape
    group_rows, heads = attn_out.shape
    own_features = weight_codes.shape[1]
    half = heads // PAIR
    layer_features = PAIR * own_features
    scaling = 1.0 / math.sqrt(group_rows * n_dp)

    dp, mp = lax.axis_index("dp"), lax.axis_index("mp")
    layer, side = dp // PAIR, dp % PAIR

    across = [(i, i ^ 1) for i in range(n_dp)]

    def layer_moves(step, keep=lambda z: True):
        return [
            (z * PAIR + x, (z + step) * PAIR + x)
            for z in range(layers)
            for x in range(PAIR)
            if 0 <= z + step < layers and keep(z)
        ]

    def swap_x(piece):
        return lax.ppermute(piece, "dp", across)

    def swap_mp(piece, bit):
        return lax.ppermute(piece, "mp", [(i, i ^ bit) for i in range(n_mp)])

    slots = []
    for r in range(layers):
        piece = lax.dynamic_slice_in_dim(
            grad_out, ((layer + r) % layers) * layer_features, layer_features, 1
        )
        if r:
            piece = lax.ppermute(
                piece,
                "dp",
                [
                    (z * PAIR + x, ((z + r) % layers) * PAIR + x)
                    for z in range(layers)
                    for x in range(PAIR)
                ],
            )
        slots.append(piece)
    own = jnp.stack(slots)

    by_token = attn_out.reshape((2,) * bits + (rows, heads))
    by_token = by_own_bits(by_token, mp, 0, bits).reshape(group_rows, heads)
    attn_own = lax.dynamic_slice_in_dim(by_token, side * half, half, 1)
    attn_other = swap_x(lax.dynamic_slice_in_dim(by_token, (1 - side) * half, half, 1))
    attn_layer = jnp.concatenate([attn_own, attn_other], 0)

    weight = dequantize(weight_codes, block_scales)
    weight_own = lax.dynamic_slice_in_dim(weight, side * half, half, 0)
    weight_other = swap_x(lax.dynamic_slice_in_dim(weight, (1 - side) * half, half, 0))
    weight_slab = halves(weight_own, weight_other, side, 1)

    own, attn_layer, weight_slab = lax.optimization_barrier((own, attn_layer, weight_slab))
    top = n_mp // 2
    via_x = swap_x(own)
    via_mp = swap_mp(own, top)
    mixed = []
    for i in range(n_dp):
        for j in range(n_mp):
            there = ((i ^ 1), j) if j % 2 == 0 else (i, j ^ top)
            mixed.append((i * n_mp + j, there[0] * n_mp + there[1]))
    far = lax.ppermute(jnp.where(mp % 2 == 0, via_mp, via_x), ("dp", "mp"), mixed)
    gathered = jnp.stack([jnp.stack([own, via_mp], 1), jnp.stack([via_x, far], 1)], 1)
    for k in range(1, bits):
        bit = top >> k
        gathered = jnp.stack([gathered, swap_mp(gathered, bit)], 2 + k)
    layer_rows = PAIR * group_rows
    columns = gathered.reshape(layers, layer_rows, layer_features)

    up, down = [attn_layer], [attn_layer]
    for r in range(1, layers):
        up.append(lax.ppermute(up[-1], "dp", layer_moves(1, lambda z: z >= r - 1)))
        down.append(lax.ppermute(down[-1], "dp", layer_moves(-1, lambda z: z <= layers - r)))

    def terms(r):
        return lax.dot_general(
            columns[r], weight_slab, (((1,), (1,)), ((), ())), preferred_element_type=jnp.float32
        )

    parts = [terms(r) for r in range(layers)]
    carried = jnp.bfloat16 if layers <= 4 else jnp.float32
    from_below = from_above = None
    for k in range(1, layers):
        send_up, send_down = parts[k], parts[layers - k]
        if k > 1:
            send_up = send_up + from_below.astype(jnp.float32)
            send_down = send_down + from_above.astype(jnp.float32)
        send_up, send_down, up[k], down[k] = lax.optimization_barrier(
            (send_up.astype(carried), send_down.astype(carried), up[k], down[k])
        )
        from_below = lax.ppermute(send_up, "dp", layer_moves(1, lambda z: z <= k - 1))
        from_above = lax.ppermute(send_down, "dp", layer_moves(-1, lambda z: z >= layers - k))
    total = None
    for r in range(layers):
        rows_r = attn_layer if r == 0 else jnp.where(layer >= r, up[r], down[layers - r])
        term = lax.dot_general(
            columns[r], rows_r, (((0,), (0,)), ((), ())), preferred_element_type=jnp.float32
        )
        total = term if total is None else total + term
    gw = (scaling * total).astype(jnp.bfloat16)
    gw_own = lax.dynamic_slice_in_dim(gw, side * own_features, own_features, 0)
    gw_other = swap_x(lax.dynamic_slice_in_dim(gw, (1 - side) * own_features, own_features, 0))
    grad_weight_t = halves(gw_own, gw_other, side, 1)

    ga = parts[0] + from_below.astype(jnp.float32) + from_above.astype(jnp.float32)
    ga = ga.astype(jnp.bfloat16)
    ga_other = swap_x(ga[group_rows:])
    grad_attn = halves(ga[:group_rows], ga_other, side, 1)
    grad_attn = by_own_bits(grad_attn.reshape((2,) * bits + (rows, heads)), mp, 0, bits)
    return grad_attn.reshape(group_rows, heads), grad_weight_t


def solution(mesh):
    placed = (P(("dp", "mp"), None), P("dp", "mp"), P("mp", "dp"), P("mp", "dp"))
    return jax.shard_map(
        body, mesh=mesh, in_specs=placed, out_specs=(P("dp", "mp"), P("dp", "mp")), check_vma=False
    )
```

```python
import math

import jax
import jax.numpy as jnp
from jax import lax
from jax.sharding import PartitionSpec as P

BLOCK = 32
PAIR = 2
LINE = 4
STREAMS = 2


def dequantize(codes_part, scales_part):
    expanded = jnp.repeat(scales_part.astype(jnp.float32), BLOCK, axis=0)
    return (codes_part.astype(jnp.float32) * expanded).astype(jnp.bfloat16)


def halves(own, other, side, axis):
    first = jnp.where(side == 0, own, other)
    second = jnp.where(side == 0, other, own)
    return jnp.concatenate([first, second], axis)


def pair(own, other, side, axis):
    return halves(jnp.expand_dims(own, axis), jnp.expand_dims(other, axis), side, axis)


def together(*arrays):
    return lax.optimization_barrier(arrays)


def by_feature(rows, weight):
    return lax.dot_general(
        rows, weight, (((1,), (1,)), ((), ())), preferred_element_type=jnp.float32
    )


def by_token(columns, rows):
    return lax.dot_general(
        columns, rows, (((0,), (0,)), ((), ())), preferred_element_type=jnp.float32
    )


def body(grad_out, attn_out, weight_codes, block_scales):
    n_dp, n_mp = lax.axis_size("dp"), lax.axis_size("mp")
    layers = n_dp // PAIR
    bits = n_mp.bit_length() - 1
    group_rows, heads = attn_out.shape
    own_features = weight_codes.shape[1]
    half = heads // PAIR
    layer_rows, layer_features = PAIR * group_rows, PAIR * own_features
    scaling = 1.0 / math.sqrt(group_rows * n_dp)

    dp, mp = lax.axis_index("dp"), lax.axis_index("mp")
    layer, side = dp // PAIR, dp % PAIR
    middle = (layer > 0) & (layer < layers - 1)

    def swap_x(piece):
        return lax.ppermute(piece, "dp", [(i, i ^ 1) for i in range(n_dp)])

    def swap_mp(piece, bit):
        return lax.ppermute(piece, "mp", [(i, i ^ bit) for i in range(n_mp)])

    def move_layers(piece, to):
        moves = [(i, to(i // PAIR) * PAIR + i % PAIR) for i in range(n_dp)]
        return lax.ppermute(piece, "dp", moves)

    def outer(piece):
        return move_layers(piece, lambda z: z ^ 1)

    between = []
    for i in range(n_dp):
        z, x = i // PAIR, i % PAIR
        for j in range(n_mp):
            if z in (0, layers - 1):
                there = i, j ^ 1
            else:
                there = (((z - 1) ^ 1) + 1) * PAIR + x, j
            between.append((i * n_mp + j, there[0] * n_mp + there[1]))

    def inner(piece):
        return lax.ppermute(piece, ("dp", "mp"), between)

    slots = []
    for s in range(layers):
        piece = lax.dynamic_slice_in_dim(
            grad_out, (layer ^ s) * layer_features, layer_features, 1
        )
        slots.append(move_layers(piece, lambda z: z ^ s) if s else piece)
    own = jnp.stack(slots)

    width = half // STREAMS
    attn = []
    for k in range(STREAMS):
        keep = lax.dynamic_slice_in_dim(attn_out, side * half + k * width, width, 1)
        send = lax.dynamic_slice_in_dim(attn_out, (1 - side) * half + k * width, width, 1)
        attn.append([keep, swap_x(send)])
    weight = dequantize(weight_codes, block_scales)
    weight_own = lax.dynamic_slice_in_dim(weight, side * half, half, 0)
    weight_send = lax.dynamic_slice_in_dim(weight, (1 - side) * half, half, 0)

    top = n_mp // 2
    weight_other = swap_x(weight_send)
    own, attn[0][1], attn[-1][1], weight_other = together(
        own, attn[0][1], attn[-1][1], weight_other
    )
    via_x, via_mp = swap_x(own), swap_mp(own, top)
    attn = [jnp.concatenate(parts, 0) for parts in attn]
    if layers == LINE:
        attn_1 = [outer(a) for a in attn]
        attn_in = [inner(a) for a in attn]
    if layers == LINE:
        via_x, via_mp, attn_1[0], attn_in[0] = together(via_x, via_mp, attn_1[0], attn_in[0])
    mixed = []
    for i in range(n_dp):
        for j in range(n_mp):
            there = ((i ^ 1), j) if j % 2 == 0 else (i, j ^ top)
            mixed.append((i * n_mp + j, there[0] * n_mp + there[1]))
    far = lax.ppermute(jnp.where(mp % 2 == 0, via_mp, via_x), ("dp", "mp"), mixed)
    near = pair(own, via_mp, mp // top, 1)
    away = pair(via_x, far, mp // top, 1)
    held = jnp.stack([near, away], 1)
    if layers == LINE:
        held, attn_1, attn_in = together(held, attn_1, attn_in)
    for k in range(1, bits):
        bit = top >> k
        held = pair(held, swap_mp(held, bit), (mp // bit) % 2, 2 + k)
    cols = held.reshape(layers, layer_rows, layer_features)
    weight_slab = halves(weight_own, weight_other, side, 1)

    def terms(k):
        stream = weight_slab[k * width : (k + 1) * width]
        return by_feature(cols.reshape(-1, layer_features), stream)

    gws, gas = [], []
    if layers == LINE:
        streams = range(STREAMS)
        part = [terms(k).reshape(layers, layer_rows, width) for k in streams]
        outer_2, inner_2, outer_3, inner_3 = [], [], [], []
        for k in streams:
            send = jnp.where(middle, attn_in[k], part[k][3].astype(jnp.bfloat16))
            outer_2.append(outer(send))
            inner_2.append(inner(attn_1[k]))
        for k in streams:
            send_outer = jnp.where(middle, inner_2[k], part[k][2].astype(jnp.bfloat16))
            send_inner = (part[k][2] + outer_2[k].astype(jnp.float32)).astype(jnp.bfloat16)
            send_outer, send_inner = together(send_outer, send_inner)
            outer_3.append(outer(send_outer))
            inner_3.append(inner(send_inner))
        for k in streams:
            send_inner = (part[k][3] + outer_3[k].astype(jnp.float32)).astype(jnp.bfloat16)
            send_outer = part[k][1] + jnp.where(middle, inner_3[k].astype(jnp.float32), 0.0)
            send_outer, send_inner = together(send_outer.astype(jnp.bfloat16), send_inner)
            outer_4, inner_4 = outer(send_outer), inner(send_inner)
            ga = part[k][0] + outer_4.astype(jnp.float32)
            gas.append(ga + jnp.where(middle, inner_4.astype(jnp.float32), 0.0))

            attn_2 = jnp.where(middle, inner_2[k], outer_2[k])
            attn_3 = jnp.where(middle, attn_in[k], outer_3[k])
            total = by_token(cols[0], attn[k]) + by_token(cols[1], attn_1[k])
            gws.append(total + by_token(cols[2], attn_2) + by_token(cols[3], attn_3))
    else:
        lines = [[z * PAIR + x for z in range(layers)] for x in range(PAIR)]
        cols = cols[jnp.arange(layers) ^ layer].reshape(-1, layer_features)
        for k in range(STREAMS):
            attn_all = lax.all_gather(
                attn[k], "dp", axis=0, tiled=True, axis_index_groups=lines
            )
            gws.append(by_token(cols, attn_all))
            gas.append(
                lax.psum_scatter(
                    terms(k), "dp", scatter_dimension=0, tiled=True, axis_index_groups=lines
                )
            )

    gw_own, gw_other, ga_own, ga_other = [], [], [], []
    for k in range(STREAMS):
        gw = (scaling * gws[k]).astype(jnp.bfloat16)
        send = lax.dynamic_slice_in_dim(gw, (1 - side) * own_features, own_features, 0)
        gw_own.append(lax.dynamic_slice_in_dim(gw, side * own_features, own_features, 0))
        gw_other.append(swap_x(send))
        ga = gas[k].astype(jnp.bfloat16)
        ga_own.append(ga[:group_rows])
        ga_other.append(swap_x(ga[group_rows:]))
    beside = lambda parts: jnp.concatenate(parts, 1)
    grad_weight_t = halves(beside(gw_own), beside(gw_other), side, 1)
    grad_attn = halves(beside(ga_own), beside(ga_other), side, 1)
    return grad_attn, grad_weight_t


def solution(mesh):
    placed = (P(("dp", "mp"), None), P("dp", "mp"), P("mp", "dp"), P("mp", "dp"))
    return jax.shard_map(
        body, mesh=mesh, in_specs=placed, out_specs=(P("dp", "mp"), P("dp", "mp")), check_vma=False
    )
```

```python
import math

import jax
import jax.numpy as jnp
from jax import lax
from jax.sharding import PartitionSpec as P

BLOCK = 32
PAIR = 2
LINE = 4


def dequantize(codes_part, scales_part):
    expanded = jnp.repeat(scales_part.astype(jnp.float32), BLOCK, axis=0)
    return (codes_part.astype(jnp.float32) * expanded).astype(jnp.bfloat16)


def halves(own, other, side, axis):
    first = jnp.where(side == 0, own, other)
    second = jnp.where(side == 0, other, own)
    return jnp.concatenate([first, second], axis)


def pair(own, other, side, axis):
    return halves(jnp.expand_dims(own, axis), jnp.expand_dims(other, axis), side, axis)


def together(*arrays):
    return lax.optimization_barrier(arrays)


def by_feature(rows, weight):
    return lax.dot_general(
        rows, weight, (((1,), (1,)), ((), ())), preferred_element_type=jnp.float32
    )


def by_token(columns, rows):
    return lax.dot_general(
        columns, rows, (((0,), (0,)), ((), ())), preferred_element_type=jnp.float32
    )


def body(grad_out, attn_out, weight_codes, block_scales):
    n_dp, n_mp = lax.axis_size("dp"), lax.axis_size("mp")
    layers = n_dp // PAIR
    bits = n_mp.bit_length() - 1
    group_rows, heads = attn_out.shape
    own_features = weight_codes.shape[1]
    half = heads // PAIR
    layer_features = PAIR * own_features
    scaling = 1.0 / math.sqrt(group_rows * n_dp)

    dp, mp = lax.axis_index("dp"), lax.axis_index("mp")
    layer, side = dp // PAIR, dp % PAIR
    middle = (layer > 0) & (layer < layers - 1)

    def swap_x(piece):
        return lax.ppermute(piece, "dp", [(i, i ^ 1) for i in range(n_dp)])

    def with_mp(piece, k):
        bit = n_mp >> (k + 1)
        other = lax.ppermute(piece, "mp", [(i, i ^ bit) for i in range(n_mp)])
        return pair(piece, other, (mp // bit) % 2, 1 + k)

    def move_layers(piece, to):
        moves = [(i, to(i // PAIR) * PAIR + i % PAIR) for i in range(n_dp)]
        return lax.ppermute(piece, "dp", moves)

    def outer(piece):
        return move_layers(piece, lambda z: z ^ 1)

    between = []
    for i in range(n_dp):
        z, x = i // PAIR, i % PAIR
        for j in range(n_mp):
            if z in (0, layers - 1):
                there = i, j ^ 1
            else:
                there = (((z - 1) ^ 1) + 1) * PAIR + x, j
            between.append((i * n_mp + j, there[0] * n_mp + there[1]))

    def inner(piece):
        return lax.ppermute(piece, ("dp", "mp"), between)

    slots = []
    for s in range(layers):
        piece = lax.dynamic_slice_in_dim(
            grad_out, (layer ^ s) * layer_features, layer_features, 1
        )
        slots.append(move_layers(piece, lambda z: z ^ s) if s else piece)
    held = jnp.stack(slots)

    attn_own = lax.dynamic_slice_in_dim(attn_out, side * half, half, 1)
    attn_other = swap_x(lax.dynamic_slice_in_dim(attn_out, (1 - side) * half, half, 1))
    weight = dequantize(weight_codes, block_scales)
    weight_other = swap_x(weight)
    weight_slab = halves(weight, weight_other, side, 1)

    held, attn_other = together(held, attn_other)
    attn = jnp.stack([attn_own, attn_other])
    if layers == LINE:
        attn_1, attn_in = outer(attn), inner(attn)

    for k in range(bits - 1):
        held = with_mp(held, k)
    cols = with_mp(held, bits - 1).reshape(layers, group_rows, layer_features)
    held_other = swap_x(held)
    cols_other = with_mp(held_other, bits - 1).reshape(cols.shape)

    def terms(k):
        stream = weight_slab[k * half : (k + 1) * half]
        part = by_feature(cols.reshape(-1, layer_features), stream)
        return part.reshape(layers, group_rows, half)

    streams = range(PAIR)
    part = [terms(k) for k in streams]
    if layers == LINE:
        outer_2, inner_2, outer_3, inner_3, gas = [], [], [], [], []
        for k in streams:
            send = jnp.where(middle, attn_in[k], part[k][3].astype(jnp.bfloat16))
            send_outer, send_inner = together(send, attn_1[k])
            outer_2.append(outer(send_outer))
            inner_2.append(inner(send_inner))
        for k in streams:
            send_outer = jnp.where(middle, inner_2[k], part[k][2].astype(jnp.bfloat16))
            send_inner = (part[k][2] + outer_2[k].astype(jnp.float32)).astype(jnp.bfloat16)
            send_outer, send_inner = together(send_outer, send_inner)
            outer_3.append(outer(send_outer))
            inner_3.append(inner(send_inner))
        for k in streams:
            send_inner = (part[k][3] + outer_3[k].astype(jnp.float32)).astype(jnp.bfloat16)
            send_outer = part[k][1] + jnp.where(middle, inner_3[k].astype(jnp.float32), 0.0)
            send_outer, send_inner = together(send_outer.astype(jnp.bfloat16), send_inner)
            outer_4, inner_4 = outer(send_outer), inner(send_inner)
            ga = part[k][0] + outer_4.astype(jnp.float32)
            gas.append(ga + jnp.where(middle, inner_4.astype(jnp.float32), 0.0))
        total = 0.0
        for k, side_cols in enumerate((cols, cols_other)):
            attn_2 = jnp.where(middle, inner_2[k], outer_2[k])
            total = total + by_token(side_cols[0], attn[k]) + by_token(side_cols[1], attn_1[k])
            total = total + by_token(side_cols[2], attn_2)
        for k, side_cols in enumerate((cols, cols_other)):
            attn_3 = jnp.where(middle, attn_in[k], outer_3[k])
            total = total + by_token(side_cols[3], attn_3)
    else:
        lines = [[z * PAIR + x for z in range(layers)] for x in range(PAIR)]
        total = 0.0
        for k, side_cols in enumerate((cols, cols_other)):
            attn_all = lax.all_gather(
                attn[k], "dp", axis=0, tiled=True, axis_index_groups=lines
            )
            ordered = side_cols[jnp.arange(layers) ^ layer].reshape(-1, layer_features)
            total = total + by_token(ordered, attn_all)
        gas = []
        for k in streams:
            ordered = part[k][jnp.arange(layers) ^ layer].reshape(-1, half)
            gas.append(
                lax.psum_scatter(
                    ordered, "dp", scatter_dimension=0, tiled=True, axis_index_groups=lines
                )
            )

    gw = (scaling * total).astype(jnp.bfloat16)
    gw_own = lax.dynamic_slice_in_dim(gw, side * own_features, own_features, 0)
    gw_other = swap_x(lax.dynamic_slice_in_dim(gw, (1 - side) * own_features, own_features, 0))
    grad_weight_t = halves(gw_own, gw_other, side, 1)
    grad_attn = jnp.concatenate(gas, 1).astype(jnp.bfloat16)
    return grad_attn, grad_weight_t


def solution(mesh):
    placed = (P(("dp", "mp"), None), P("dp", "mp"), P("mp", "dp"), P("mp", "dp"))
    return jax.shard_map(
        body, mesh=mesh, in_specs=placed, out_specs=(P("dp", "mp"), P("dp", "mp")), check_vma=False
    )
```

```python
import math

import jax
import jax.numpy as jnp
from jax import lax
from jax.experimental import pallas as pl
from jax.experimental.pallas import tpu as pltpu
from jax.sharding import PartitionSpec as P

BLOCK = 32
PAIR = 2
LINE = 4


def dequantize(codes_part, scales_part):
    expanded = jnp.repeat(scales_part.astype(jnp.float32), BLOCK, axis=0)
    return (codes_part.astype(jnp.float32) * expanded).astype(jnp.bfloat16)


def pack(side, codes, scales, attn_out):
    heads, features = codes.shape
    group_rows = attn_out.shape[0]
    count = heads // group_rows
    width = heads // PAIR // count

    def kernel(side_ref, codes_ref, scales_ref, attn_ref, out_ref):
        scale = scales_ref[...].astype(jnp.float32)
        for k in range(heads // BLOCK):
            rows = slice(k * BLOCK, (k + 1) * BLOCK)
            values = codes_ref[rows].astype(jnp.float32) * scale[k : k + 1]
            out_ref[rows, :features] = values.astype(out_ref.dtype)
        for other in range(PAIR):

            @pl.when(side_ref[0] == 1 - other)
            def _():
                for k in range(count):
                    first = other * (heads // PAIR) + k * width
                    rows = slice(k * group_rows, (k + 1) * group_rows)
                    out_ref[rows, features:] = attn_ref[:, first : first + width]

    in_vmem = pl.BlockSpec(memory_space=pltpu.VMEM)
    size = heads * (features + width)
    return pl.pallas_call(
        kernel,
        out_shape=jax.ShapeDtypeStruct((heads, features + width), codes.dtype),
        in_specs=[pl.BlockSpec(memory_space=pltpu.SMEM), in_vmem, in_vmem, in_vmem],
        out_specs=in_vmem,
        cost_estimate=pl.CostEstimate(flops=size, bytes_accessed=4 * size, transcendentals=0),
    )(side[None].astype(jnp.int32), codes, scales, attn_out)


def halves(own, other, side, axis):
    first = jnp.where(side == 0, own, other)
    second = jnp.where(side == 0, other, own)
    return jnp.concatenate([first, second], axis)


def pair(own, other, side, axis):
    return halves(jnp.expand_dims(own, axis), jnp.expand_dims(other, axis), side, axis)


def together(*arrays):
    return lax.optimization_barrier(arrays)


def by_feature(rows, weight):
    return lax.dot_general(
        rows, weight, (((1,), (1,)), ((), ())), preferred_element_type=jnp.float32
    )


def by_token(columns, rows):
    return lax.dot_general(
        columns, rows, (((0,), (0,)), ((), ())), preferred_element_type=jnp.float32
    )


def body(grad_out, attn_out, weight_codes, block_scales):
    n_dp, n_mp = lax.axis_size("dp"), lax.axis_size("mp")
    layers = n_dp // PAIR
    bits = n_mp.bit_length() - 1
    group_rows, heads = attn_out.shape
    own_features = weight_codes.shape[1]
    half = heads // PAIR
    layer_features = PAIR * own_features
    scaling = 1.0 / math.sqrt(group_rows * n_dp)

    dp, mp = lax.axis_index("dp"), lax.axis_index("mp")
    layer, side = dp // PAIR, dp % PAIR
    middle = (layer > 0) & (layer < layers - 1)

    def swap_x(piece):
        return lax.ppermute(piece, "dp", [(i, i ^ 1) for i in range(n_dp)])

    def with_mp(piece, k):
        bit = n_mp >> (k + 1)
        other = lax.ppermute(piece, "mp", [(i, i ^ bit) for i in range(n_mp)])
        return pair(piece, other, (mp // bit) % 2, 1 + k)

    def move_layers(piece, to):
        moves = [(i, to(i // PAIR) * PAIR + i % PAIR) for i in range(n_dp)]
        return lax.ppermute(piece, "dp", moves)

    def outer(piece):
        return move_layers(piece, lambda z: z ^ 1)

    between = []
    for i in range(n_dp):
        z, x = i // PAIR, i % PAIR
        for j in range(n_mp):
            if z in (0, layers - 1):
                there = i, j ^ 1
            else:
                there = (((z - 1) ^ 1) + 1) * PAIR + x, j
            between.append((i * n_mp + j, there[0] * n_mp + there[1]))

    def inner(piece):
        return lax.ppermute(piece, ("dp", "mp"), between)

    slots = []
    for s in range(layers):
        piece = lax.dynamic_slice_in_dim(
            grad_out, (layer ^ s) * layer_features, layer_features, 1
        )
        slots.append(move_layers(piece, lambda z: z ^ s) if s else piece)
    held = jnp.stack(slots)

    attn_own = lax.dynamic_slice_in_dim(attn_out, side * half, half, 1)
    packed = heads % group_rows == 0
    if packed:
        sent = pack(side, weight_codes, block_scales, attn_out)
        weight = sent[:, :own_features]
        got = [swap_x(sent)]
    else:
        weight = dequantize(weight_codes, block_scales)
        attn_send = lax.dynamic_slice_in_dim(attn_out, (1 - side) * half, half, 1)
        got = [swap_x(weight), swap_x(attn_send)]

    if layers == LINE:
        attn_1, attn_in = [outer(attn_own)], [inner(attn_own)]

    for k in range(bits - 1):
        held = with_mp(held, k)
    if layers == LINE:
        held, attn_1[0], attn_in[0] = together(held, attn_1[0], attn_in[0])
    held, got = together(held, got)
    if packed:
        weight_other, blocks = got[0][:, :own_features], got[0][:, own_features:]
        attn_other = jnp.concatenate(jnp.split(blocks, heads // group_rows), 1)
    else:
        weight_other, attn_other = got
    attn = [attn_own, attn_other]
    if layers == LINE:
        attn_1.append(outer(attn_other))
        attn_in.append(inner(attn_other))
    cols = with_mp(held, bits - 1).reshape(layers, group_rows, layer_features)
    held_other, _ = together(held, weight_other)
    held_other = swap_x(held_other)

    weight_slab = halves(weight, weight_other, side, 1)

    def terms(k):
        stream = weight_slab[k * half : (k + 1) * half]
        part = by_feature(cols.reshape(-1, layer_features), stream)
        return part.reshape(layers, group_rows, half)

    if layers != LINE:
        cols_other = with_mp(held_other, bits - 1).reshape(cols.shape)
    streams = range(PAIR)
    part = [terms(k) for k in streams]
    if layers == LINE:
        outer_2, inner_2, outer_3, inner_3, gas = [], [], [], [], []
        before = []
        for k in streams:
            send = jnp.where(middle, attn_in[k], part[k][3].astype(jnp.bfloat16))
            send_outer, send_inner, *before = together(send, attn_1[k], *before)
            before = [send_outer, send_inner]
            outer_2.append(outer(send_outer))
            inner_2.append(inner(send_inner))
        held_other, _ = together(held_other, outer_2[0])
        cols_other = with_mp(held_other, bits - 1).reshape(cols.shape)
        before = []
        for k in streams:
            send_outer = jnp.where(middle, inner_2[k], part[k][2].astype(jnp.bfloat16))
            send_inner = (part[k][2] + outer_2[k].astype(jnp.float32)).astype(jnp.bfloat16)
            send_outer, send_inner, *before = together(send_outer, send_inner, *before)
            before = [send_outer, send_inner]
            outer_3.append(outer(send_outer))
            inner_3.append(inner(send_inner))
        before = []
        for k in streams:
            send_inner = (part[k][3] + outer_3[k].astype(jnp.float32)).astype(jnp.bfloat16)
            send_outer = part[k][1] + jnp.where(middle, inner_3[k].astype(jnp.float32), 0.0)
            send_outer = send_outer.astype(jnp.bfloat16)
            send_outer, send_inner, *before = together(send_outer, send_inner, *before)
            before = [send_outer, send_inner]
            outer_4, inner_4 = outer(send_outer), inner(send_inner)
            ga = part[k][0] + outer_4.astype(jnp.float32)
            gas.append(ga + jnp.where(middle, inner_4.astype(jnp.float32), 0.0))
        total = 0.0
        for k, side_cols in enumerate((cols, cols_other)):
            attn_2 = jnp.where(middle, inner_2[k], outer_2[k])
            total = total + by_token(side_cols[0], attn[k]) + by_token(side_cols[1], attn_1[k])
            total = total + by_token(side_cols[2], attn_2)
        for k, side_cols in enumerate((cols, cols_other)):
            attn_3 = jnp.where(middle, attn_in[k], outer_3[k])
            total = total + by_token(side_cols[3], attn_3)
    else:
        lines = [[z * PAIR + x for z in range(layers)] for x in range(PAIR)]
        total = 0.0
        for k, side_cols in enumerate((cols, cols_other)):
            attn_all = lax.all_gather(
                attn[k], "dp", axis=0, tiled=True, axis_index_groups=lines
            )
            ordered = side_cols[jnp.arange(layers) ^ layer].reshape(-1, layer_features)
            total = total + by_token(ordered, attn_all)
        gas = []
        for k in streams:
            ordered = part[k][jnp.arange(layers) ^ layer].reshape(-1, half)
            gas.append(
                lax.psum_scatter(
                    ordered, "dp", scatter_dimension=0, tiled=True, axis_index_groups=lines
                )
            )

    gw = (scaling * total).astype(jnp.bfloat16)
    gw_own = lax.dynamic_slice_in_dim(gw, side * own_features, own_features, 0)
    gw_other = swap_x(lax.dynamic_slice_in_dim(gw, (1 - side) * own_features, own_features, 0))
    grad_weight_t = halves(gw_own, gw_other, side, 1)
    grad_attn = jnp.concatenate(gas, 1).astype(jnp.bfloat16)
    return grad_attn, grad_weight_t


def solution(mesh):
    placed = (P(("dp", "mp"), None), P("dp", "mp"), P("mp", "dp"), P("mp", "dp"))
    return jax.shard_map(
        body, mesh=mesh, in_specs=placed, out_specs=(P("dp", "mp"), P("dp", "mp")), check_vma=False
    )
```

```python
import math

import jax
import jax.numpy as jnp
from jax import lax
from jax.experimental import pallas as pl
from jax.experimental.pallas import tpu as pltpu
from jax.sharding import PartitionSpec as P

BLOCK = 32
PAIR = 2
LINE = 4
STEPS = 2


def dequantize(codes_part, scales_part):
    expanded = jnp.repeat(scales_part.astype(jnp.float32), BLOCK, axis=0)
    return (codes_part.astype(jnp.float32) * expanded).astype(jnp.bfloat16)


def pack(side, codes, scales, attn_out):
    heads, features = codes.shape
    group_rows = attn_out.shape[0]
    blocks = heads // group_rows // STEPS
    width = group_rows // PAIR
    rows = heads // STEPS

    def kernel(side_ref, codes_ref, scales_ref, attn_ref, out_ref):
        scale = scales_ref[...].astype(jnp.float32)
        for k in range(rows // BLOCK):
            part = slice(k * BLOCK, (k + 1) * BLOCK)
            values = codes_ref[part].astype(jnp.float32) * scale[k : k + 1]
            out_ref[part, :features] = values.astype(out_ref.dtype)
        for k in range(blocks):
            part = slice(k * group_rows, (k + 1) * group_rows)
            out_ref[part, features:] = attn_ref[:, k * width : (k + 1) * width]

    size = heads * (features + width)
    return pl.pallas_call(
        kernel,
        out_shape=jax.ShapeDtypeStruct((heads, features + width), codes.dtype),
        grid_spec=pltpu.PrefetchScalarGridSpec(
            num_scalar_prefetch=1,
            grid=(STEPS,),
            in_specs=[
                pl.BlockSpec((rows, features), lambda i, side_ref: (i, 0)),
                pl.BlockSpec((rows // BLOCK, features), lambda i, side_ref: (i, 0)),
                pl.BlockSpec(
                    (group_rows, blocks * width), lambda i, side_ref: (0, (1 - side_ref[0]) * STEPS + i)
                ),
            ],
            out_specs=pl.BlockSpec((rows, features + width), lambda i, side_ref: (i, 0)),
        ),
        cost_estimate=pl.CostEstimate(flops=size, bytes_accessed=4 * size, transcendentals=0),
    )(side[None].astype(jnp.int32), codes, scales, attn_out)


def halves(own, other, side, axis):
    first = jnp.where(side == 0, own, other)
    second = jnp.where(side == 0, other, own)
    return jnp.concatenate([first, second], axis)


def pair(own, other, side, axis):
    return halves(jnp.expand_dims(own, axis), jnp.expand_dims(other, axis), side, axis)


def together(*arrays):
    return lax.optimization_barrier(arrays)


def by_feature(rows, weight):
    return lax.dot_general(
        rows, weight, (((1,), (1,)), ((), ())), preferred_element_type=jnp.float32
    )


def by_token(columns, rows):
    return lax.dot_general(
        columns, rows, (((0,), (0,)), ((), ())), preferred_element_type=jnp.float32
    )


def body(grad_out, attn_out, weight_codes, block_scales):
    n_dp, n_mp = lax.axis_size("dp"), lax.axis_size("mp")
    layers = n_dp // PAIR
    bits = n_mp.bit_length() - 1
    group_rows, heads = attn_out.shape
    own_features = weight_codes.shape[1]
    half = heads // PAIR
    layer_features = PAIR * own_features
    scaling = 1.0 / math.sqrt(group_rows * n_dp)

    dp, mp = lax.axis_index("dp"), lax.axis_index("mp")
    layer, side = dp // PAIR, dp % PAIR
    middle = (layer > 0) & (layer < layers - 1)

    def swap_x(piece):
        return lax.ppermute(piece, "dp", [(i, i ^ 1) for i in range(n_dp)])

    def with_mp(piece, k):
        bit = n_mp >> (k + 1)
        other = lax.ppermute(piece, "mp", [(i, i ^ bit) for i in range(n_mp)])
        return pair(piece, other, (mp // bit) % 2, 1 + k)

    def move_layers(piece, to):
        moves = [(i, to(i // PAIR) * PAIR + i % PAIR) for i in range(n_dp)]
        return lax.ppermute(piece, "dp", moves)

    def outer(piece):
        return move_layers(piece, lambda z: z ^ 1)

    between = []
    for i in range(n_dp):
        z, x = i // PAIR, i % PAIR
        for j in range(n_mp):
            if z in (0, layers - 1):
                there = i, j ^ 1
            else:
                there = (((z - 1) ^ 1) + 1) * PAIR + x, j
            between.append((i * n_mp + j, there[0] * n_mp + there[1]))

    def inner(piece):
        return lax.ppermute(piece, ("dp", "mp"), between)

    slots = []
    for s in range(layers):
        piece = lax.dynamic_slice_in_dim(
            grad_out, (layer ^ s) * layer_features, layer_features, 1
        )
        slots.append(move_layers(piece, lambda z: z ^ s) if s else piece)
    held = jnp.stack(slots)

    attn_own = lax.dynamic_slice_in_dim(attn_out, side * half, half, 1)
    packed = heads % (STEPS * group_rows) == 0
    if packed:
        sent = pack(side, weight_codes, block_scales, attn_out)
        weight = sent[:, :own_features]
        got = [swap_x(sent)]
    else:
        weight = dequantize(weight_codes, block_scales)
        attn_send = lax.dynamic_slice_in_dim(attn_out, (1 - side) * half, half, 1)
        got = [swap_x(weight), swap_x(attn_send)]

    if layers == LINE:
        attn_1, attn_in = [outer(attn_own)], [inner(attn_own)]

    for k in range(bits - 1):
        held = with_mp(held, k)
    if layers == LINE:
        held, attn_1[0], attn_in[0] = together(held, attn_1[0], attn_in[0])
    held, got = together(held, got)
    if packed:
        weight_other, blocks = got[0][:, :own_features], got[0][:, own_features:]
        attn_other = jnp.concatenate(jnp.split(blocks, heads // group_rows), 1)
    else:
        weight_other, attn_other = got
    attn = [attn_own, attn_other]
    if layers == LINE:
        attn_1.append(outer(attn_other))
        attn_in.append(inner(attn_other))
    cols = with_mp(held, bits - 1).reshape(layers, group_rows, layer_features)
    held_other, _ = together(held, weight_other)
    held_other = swap_x(held_other)

    weight_slab = halves(weight, weight_other, side, 1)

    def terms(k):
        stream = weight_slab[k * half : (k + 1) * half]
        part = by_feature(cols.reshape(-1, layer_features), stream)
        return part.reshape(layers, group_rows, half)

    if layers != LINE:
        cols_other = with_mp(held_other, bits - 1).reshape(cols.shape)
    streams = range(PAIR)
    part = [terms(k) for k in streams]
    if layers == LINE:
        outer_2, inner_2, outer_3, inner_3, gas = [], [], [], [], []
        before = []
        for k in streams:
            send = jnp.where(middle, attn_in[k], part[k][3].astype(jnp.bfloat16))
            send_outer, send_inner, *before = together(send, attn_1[k], *before)
            before = [send_outer, send_inner]
            outer_2.append(outer(send_outer))
            inner_2.append(inner(send_inner))
        held_other, _ = together(held_other, outer_2[0])
        cols_other = with_mp(held_other, bits - 1).reshape(cols.shape)
        before = []
        for k in streams:
            send_outer = jnp.where(middle, inner_2[k], part[k][2].astype(jnp.bfloat16))
            send_inner = (part[k][2] + outer_2[k].astype(jnp.float32)).astype(jnp.bfloat16)
            send_outer, send_inner, *before = together(send_outer, send_inner, *before)
            before = [send_outer, send_inner]
            outer_3.append(outer(send_outer))
            inner_3.append(inner(send_inner))
        total, partial = 0.0, []
        for k, side_cols in enumerate((cols, cols_other)):
            attn_2 = jnp.where(middle, inner_2[k], outer_2[k])
            sums = by_token(side_cols[0], attn[k]) + by_token(side_cols[1], attn_1[k])
            partial.append(sums + by_token(side_cols[2], attn_2))
        outer_3[1], inner_3[1], partial = together(outer_3[1], inner_3[1], partial)
        before = []
        for k in streams:
            send_inner = (part[k][3] + outer_3[k].astype(jnp.float32)).astype(jnp.bfloat16)
            send_outer = part[k][1] + jnp.where(middle, inner_3[k].astype(jnp.float32), 0.0)
            send_outer = send_outer.astype(jnp.bfloat16)
            send_outer, send_inner, *before = together(send_outer, send_inner, *before)
            before = [send_outer, send_inner]
            outer_4, inner_4 = outer(send_outer), inner(send_inner)
            ga = part[k][0] + outer_4.astype(jnp.float32)
            gas.append(ga + jnp.where(middle, inner_4.astype(jnp.float32), 0.0))
        total = partial[0] + partial[1]
        for k, side_cols in enumerate((cols, cols_other)):
            attn_3 = jnp.where(middle, attn_in[k], outer_3[k])
            total = total + by_token(side_cols[3], attn_3)
    else:
        lines = [[z * PAIR + x for z in range(layers)] for x in range(PAIR)]
        total = 0.0
        for k, side_cols in enumerate((cols, cols_other)):
            attn_all = lax.all_gather(
                attn[k], "dp", axis=0, tiled=True, axis_index_groups=lines
            )
            ordered = side_cols[jnp.arange(layers) ^ layer].reshape(-1, layer_features)
            total = total + by_token(ordered, attn_all)
        gas = []
        for k in streams:
            ordered = part[k][jnp.arange(layers) ^ layer].reshape(-1, half)
            gas.append(
                lax.psum_scatter(
                    ordered, "dp", scatter_dimension=0, tiled=True, axis_index_groups=lines
                )
            )

    gw = (scaling * total).astype(jnp.bfloat16)
    gw_own = lax.dynamic_slice_in_dim(gw, side * own_features, own_features, 0)
    gw_other = swap_x(lax.dynamic_slice_in_dim(gw, (1 - side) * own_features, own_features, 0))
    grad_weight_t = halves(gw_own, gw_other, side, 1)
    grad_attn = jnp.concatenate(gas, 1).astype(jnp.bfloat16)
    return grad_attn, grad_weight_t


def solution(mesh):
    placed = (P(("dp", "mp"), None), P("dp", "mp"), P("mp", "dp"), P("mp", "dp"))
    return jax.shard_map(
        body, mesh=mesh, in_specs=placed, out_specs=(P("dp", "mp"), P("dp", "mp")), check_vma=False
    )
```
